512 devices in a mesh: patch: 64 (over z, x_lo, core), img: 8 (over y, x_hi).
Axes of the slice: x: 4 (x_hi: 2, x_lo: 2; x = x_hi * 2 + x_lo), y: 4, z: 16, core: 2. Of those that a mesh axis runs over, the one named last changes fastest.
Arguments:
- latents: bfloat16 [65536, 640], P(('img', 'patch')), parts along dimension 0, may hold values from -16 to 16
- stale_keys: bfloat16 [65536, 320], P(('img', 'patch')), parts along dimension 0, may hold values from -6 to 6
- stale_values: bfloat16 [65536, 320], P(('img', 'patch')), parts along dimension 0, may hold values from -6 to 6
- timestep: int32 [1], replicated, may hold values from 0 to 999
- text_ids: int32 [616], P('img'), parts along dimension 0, may hold values from 0 to 24703
- text_table: bfloat16 [24704, 1280], P('patch'), may hold values from -24 to 24
- time_weight: bfloat16 [1280, 640], replicated, may hold values from -0.15625 to 0.15625
- norm_gain: float32 [640], replicated, may hold values from 0.5 to 1.5
- norm_bias: float32 [640], replicated, may hold values from -3 to 3
- w_query: bfloat16 [640, 320], replicated, may hold values from -0.25 to 0.25
- w_key: bfloat16 [640, 320], replicated, may hold values from -0.25 to 0.25
- w_value: bfloat16 [640, 320], replicated, may hold values from -0.25 to 0.25
- w_out: bfloat16 [320, 640], replicated, may hold values from -1.25 to 1.25
Outputs:
- mixed: bfloat16 [65536, 640], P(('img', 'patch')), parts along dimension 0
- fresh_keys: bfloat16 [65536, 320], P(('img', 'patch')), parts along dimension 0
- fresh_values: bfloat16 [65536, 320], P(('img', 'patch')), parts along dimension 0
The draws below stay inside these ranges and needn't reach their ends.
There are 8 independent parts, one for each index of `img`. The reference program is written for one: setup_inputs(seed, part) draws one part's arguments, and reference() takes and returns one part's arrays. A program takes and returns all parts, laid end to end along the dimension named above; an argument that names none is the same for every part. Nothing has to cross between parts.
All inputs are finite; a program needn't handle non-finite values.
Results may differ from the reference program's by a relative error of at most 0.0051.
Values may be sent and summed in bfloat16 or wider, within the bound.
A program may use at most 128 MiB of HBM per device.

```python
import math
import jax
import jax.numpy as jnp
import numpy as np
from jax import lax

D = 640
HEADS = 5
HEAD_DIM = 64
GROUPS = 32
TEMB = 1280
VOCAB = 24704
TEXT = 77
TOK_DEV = 128
ATT = 320
TOKENS = 8192
N_PATCH = 64


def draw_latents(key, part):
    key = jax.random.fold_in(key, 11)
    noise_key, amp_key, sign_key = jax.random.split(key, 3)
    position = jnp.arange(TOKENS, dtype=jnp.float32) / max(TOKENS - 1, 1)
    signs = jnp.where(jax.random.bernoulli(sign_key, 0.5, (D,)), 1.0, -1.0).astype(jnp.float32)
    noise = jnp.clip(jax.random.normal(noise_key, (TOKENS, D), jnp.float32), -6.0, 6.0)
    amps = jax.random.uniform(amp_key, (D,), jnp.float32, 0.5, 1.5) * signs
    ramp = 1.0 + 2.0 * position
    values = noise + ramp[:, None] * amps[None, :]
    return values.astype(jnp.bfloat16)


def set_ends(result, stream_key, smallest, largest):
    place = [jax.random.randint(jax.random.fold_in(stream_key, axis), (), 0, length) for axis, length in enumerate(result.shape)]
    widest = result.shape.index(max(result.shape))
    next_to = place[:widest] + [(place[widest] + 1) % result.shape[widest]] + place[widest + 1:]
    return result.at[tuple(place)].set(smallest).at[tuple(next_to)].set(largest)


def levels(stream_key, shape, pieces, low, largest):
    def one(axis_at, shards_of):
        draws = jax.random.uniform(jax.random.fold_in(jax.random.fold_in(stream_key, 6), axis_at), (shards_of,), jnp.float32, low / len(pieces), largest / len(pieces))
        return jnp.repeat(jnp.exp(draws), shape[axis_at] // shards_of).reshape((-1,) + (1,) * (len(shape) - axis_at - 1))

    level = one(*pieces[0])
    for cut in pieces[1:]:
        level = level * one(*cut)
    return level


def rank_bounds(amount, slope):
    weights = [(1 << 20) // math.isqrt(grade ** slope) + 1 for grade in range(1, amount + 1)]
    spread = 1 + sum(weights) // (1 << 30)
    return np.cumsum(np.array([max(1, weight // spread) for weight in weights]))


def skewed_ids(stream_key, dims, count, lean):
    listing = rank_bounds(count, lean)
    lot = jax.random.randint(jax.random.fold_in(stream_key, 1), dims, 0, int(listing[count - 1]))
    rank = jnp.searchsorted(jnp.asarray(listing, jnp.int32), lot, side="right")
    return jax.random.permutation(jax.random.fold_in(stream_key, 2), count)[rank].astype(jnp.int32)


def centred(key, extent, scale, reach, shards=(), kind=jnp.bfloat16):
    result = jax.random.normal(key, extent, jnp.float32) * scale
    if len(shards) > 0:
        result = levels(key, extent, shards, -0.22, 0.18) * result
    return jnp.clip(result, min=-reach, max=reach).astype(kind)


def setup_inputs(seed: int = 0, part: int = 0) -> dict:
    seeds = jax.random.split(jax.random.key(seed), 14)
    part_keys = jax.random.split(jax.random.fold_in(seeds[13], part), 14)
    latents = draw_latents(jax.random.fold_in(jax.random.fold_in(seeds[13], part), 71), part)
    stale_keys = centred(part_keys[1], (TOKENS, ATT), 1.0, 6.0, ((0, 64),))
    stale_values = centred(part_keys[2], (TOKENS, ATT), 1.0, 6.0, ((0, 64),))
    timestep = jax.random.randint(seeds[3], (1,), 0, 1000).astype(jnp.int32)
    text_ids = set_ends(skewed_ids(part_keys[4], (TEXT,), VOCAB, 2), jax.random.fold_in(part_keys[4], 3), 0, VOCAB - 1).astype(jnp.int32)
    text_table = centred(seeds[5], (VOCAB, TEMB), 4.0, 24.0, ((0, 64),))
    time_weight = centred(seeds[6], (TEMB, D), TEMB ** -0.5, 0.15625)
    norm_gain = jnp.clip(1.0 + 0.1 * jax.random.normal(seeds[7], (D,), jnp.float32), 0.5, 1.5)
    norm_bias = centred(seeds[8], (D,), 0.5, 3.0, (), jnp.float32)
    w_query = centred(seeds[9], (D, ATT), D ** -0.5, 0.25)
    w_key = centred(seeds[10], (D, ATT), D ** -0.5, 0.25)
    w_value = centred(seeds[11], (D, ATT), D ** -0.5, 0.25)
    w_out = centred(seeds[12], (ATT, D), (ATT // 16) ** -0.5, 1.25)
    return dict(latents=latents, stale_keys=stale_keys, stale_values=stale_values, timestep=timestep, text_ids=text_ids, text_table=text_table, time_weight=time_weight, norm_gain=norm_gain, norm_bias=norm_bias, w_query=w_query, w_key=w_key, w_value=w_value, w_out=w_out)


def embed_time(timestep, width):
    half = width // 2
    freq = jnp.exp(-math.log(10000.0) * jnp.arange(half, dtype=jnp.float32) / half)
    angle = timestep[0].astype(jnp.float32) * freq
    return jnp.concatenate([jnp.cos(angle), jnp.sin(angle)])

def reference(latents, stale_keys, stale_values, timestep, text_ids, text_table, time_weight, norm_gain, norm_bias, w_query, w_key, w_value, w_out):
    temb = embed_time(timestep, TEMB)
    onehot = (text_ids[:, None] == jnp.arange(VOCAB, dtype=jnp.int32)[None, :]).astype(jnp.bfloat16)
    pooled = lax.optimization_barrier(jnp.sum(jnp.dot(onehot, text_table, preferred_element_type=jnp.float32), axis=0)) / TEXT
    cond = jax.nn.silu(temb + pooled).astype(jnp.bfloat16)
    shift = jnp.dot(cond[None, :], time_weight, preferred_element_type=jnp.float32)[0]
    shifted = latents.astype(jnp.float32) + shift[None, :]
    grouped = shifted.reshape(TOKENS, GROUPS, D // GROUPS)
    mean = lax.optimization_barrier(jnp.mean(grouped, axis=(0, 2)))
    centered = grouped - mean[None, :, None]
    var = lax.optimization_barrier(jnp.mean(centered * centered, axis=(0, 2)))
    normed = (centered / jnp.sqrt(var + 1e-05)[None, :, None]).reshape(TOKENS, D) * norm_gain + norm_bias
    normed = normed.astype(jnp.bfloat16)
    queries = jnp.dot(normed, w_query, preferred_element_type=jnp.float32).astype(jnp.bfloat16)
    fresh_keys = jnp.dot(normed, w_key, preferred_element_type=jnp.float32).astype(jnp.bfloat16)
    fresh_values = jnp.dot(normed, w_value, preferred_element_type=jnp.float32).astype(jnp.bfloat16)
    scale = 1.0 / math.sqrt(HEAD_DIM)

    def one_patch(index):
        start = (index * TOK_DEV).astype(jnp.int32)
        zero = jnp.zeros((), jnp.int32)
        query_rows = lax.dynamic_slice(queries, (start, zero), (TOK_DEV, ATT))
        own_keys = lax.dynamic_slice(fresh_keys, (start, zero), (TOK_DEV, ATT))
        own_values = lax.dynamic_slice(fresh_values, (start, zero), (TOK_DEV, ATT))
        keys = lax.dynamic_update_slice(stale_keys, own_keys, (start, zero))
        values = lax.dynamic_update_slice(stale_values, own_values, (start, zero))
        query_f = query_rows.astype(jnp.float32).reshape(TOK_DEV, HEADS, HEAD_DIM)
        key_f = keys.astype(jnp.float32).reshape(TOKENS, HEADS, HEAD_DIM)
        value_f = values.astype(jnp.float32).reshape(TOKENS, HEADS, HEAD_DIM)
        scores = jnp.einsum('qhd,khd->hqk', query_f, key_f) * scale
        probs = jax.nn.softmax(scores, axis=-1)
        out = jnp.einsum('hqk,khd->qhd', probs, value_f)
        return out.reshape(TOK_DEV, ATT)
    attended = lax.map(one_patch, jnp.arange(N_PATCH, dtype=jnp.int32))
    attended = attended.reshape(TOKENS, ATT).astype(jnp.bfloat16)
    mixed = shifted + jnp.dot(attended, w_out, preferred_element_type=jnp.float32)
    return (mixed.astype(jnp.bfloat16), fresh_keys, fresh_values)
```

```python
import functools
import math

import jax
import jax.numpy as jnp
from jax import lax
from jax.experimental import pallas as pl
from jax.experimental.pallas import tpu as pltpu
from jax.sharding import PartitionSpec as P

HEAD_DIM = 64
GROUPS = 32
QUAD = 4
LANE = 128
MESH = pl.DeviceIdType.MESH
BF16 = jnp.bfloat16
F32 = jnp.float32


def dot(a, b):
    return jnp.dot(a, b, preferred_element_type=F32)


def dot_nt(a, b):
    return lax.dot_general(a, b, (((1,), (1,)), ((), ())), preferred_element_type=F32)


def iota(shape, axis):
    return lax.broadcasted_iota(jnp.int32, shape, axis)


def eye(rows, cols, shift=0):
    return (iota((rows, cols), 0) + shift == iota((rows, cols), 1)).astype(BF16)


def pieces(x):
    high = x.astype(BF16).astype(F32)
    rest = x - high
    mid = rest.astype(BF16).astype(F32)
    return high, mid, rest - mid


def kernel(
    nz,
    text,
    time_ref,
    ids_ref,
    table_ref,
    gain_ref,
    bias_ref,
    lat_hbm,
    sk_hbm,
    sv_hbm,
    tw_hbm,
    wq_hbm,
    wk_hbm,
    wv_hbm,
    wo_hbm,
    mixed_hbm,
    fk_hbm,
    fv_hbm,
    lat,
    sk,
    tw,
    wq,
    wk,
    wv,
    wo,
    kv,
    stat,
    st1,
    st2,
    st3,
    qx,
    qp,
    acc,
    top,
    partial,
    arrived,
    fk,
    fv,
    mixed,
    group,
    in_sem,
    out_sem,
    up_send,
    up_recv,
    dn_send,
    dn_recv,
    s1_send,
    s1_recv,
    s2_send,
    s2_recv,
    s3_send,
    s3_recv,
    q_send,
    q_recv,
    o_send,
    o_recv,
):
    tok, width = lat.shape
    att = sk.shape[0]
    heads = att // HEAD_DIM
    me = lax.axis_index("patch")
    z = lax.div(me, QUAD)
    c = lax.rem(me, QUAD)

    def at(zz, cc):
        return {"patch": zz * QUAD + cc}

    def quad_to(j):
        return at(z, lax.rem(c + j, QUAD))

    def quad_from(j):
        return at(z, lax.rem(c + QUAD - j, QUAD))

    def along(j):
        return at(lax.rem(z + j, nz), c)

    def remote(src, dst, send, recv, who):
        return pltpu.make_async_remote_copy(
            src_ref=src, dst_ref=dst, send_sem=send, recv_sem=recv, device_id=who, device_id_type=MESH
        )

    loads = [
        pltpu.make_async_copy(src, dst, in_sem.at[i])
        for i, (src, dst) in enumerate(
            [
                (sk_hbm, sk),
                (sv_hbm, kv.at[0, pl.ds(att, att)]),
                (lat_hbm, lat),
                (tw_hbm, tw),
                (wq_hbm, wq),
                (wk_hbm, wk),
                (wv_hbm, wv),
                (wo_hbm, wo),
            ]
        )
    ]
    for load in loads:
        load.start()

    barrier = pltpu.get_barrier_semaphore()
    for j in range(1, QUAD):
        pl.semaphore_signal(barrier, inc=1, device_id=quad_to(j), device_id_type=MESH)
    for j in range(1, nz):
        pl.semaphore_signal(barrier, inc=1, device_id=along(j), device_id_type=MESH)

    def fill_keys(slot, keys):
        kv[slot, 0:128] = keys[:, 0:128]
        kv[slot, 128:256] = keys[:, 128:256]
        early, late = keys[0:64, 256:320], keys[64:128, 256:320]
        tail = dot(early, eye(64, LANE)) + dot(late, eye(64, LANE, 64))
        kv[slot, 256:320] = tail.astype(BF16)

    loads[0].wait()
    fill_keys(0, dot_nt(eye(tok, tok), sk[...]).astype(BF16))
    loads[1].wait()
    pl.semaphore_wait(barrier, QUAD - 1 + nz - 1)

    chunks = nz - 1
    reach = nz // 2

    def slot_up(d):
        return 0 if d == 0 else 2 * d - 1

    def slot_dn(d):
        return 0 if d == 0 else (2 * d if d < reach else 2 * d - 1)

    def ring(k, up):
        d = k // 2 + 1
        part = k % 2
        if k == chunks - 1:
            part = 0 if up else 1
        rows = pl.ds(part * att, att)
        place = slot_up if up else slot_dn
        send, recv = (up_send, up_recv) if up else (dn_send, dn_recv)
        return remote(
            kv.at[place(d - 1), rows],
            kv.at[place(d), rows],
            send.at[k],
            recv.at[k],
            along(1 if up else nz - 1),
        )

    done = [0]

    def service(count):
        for _ in range(count):
            k = done[0]
            if k >= chunks:
                return
            for up in (True, False):
                ring(k, up).wait_recv()
                if k + 2 < chunks - 1:
                    ring(k + 2, up).start()
                elif k == chunks - 3 and up or k == chunks - 2 and not up:
                    ring(chunks - 1, up).start()
            done[0] = k + 1

    def ensure(count):
        service(min(count, chunks) - done[0])

    for k in range(min(2, chunks)):
        for up in (True, False):
            ring(k, up).start()

    loads[2].wait()
    lat32 = lat[...].astype(F32)
    mean = jnp.sum(lat32, axis=0, keepdims=True) * (1.0 / tok)
    dev = lat32 - mean
    spread = jnp.sum(dev * dev, axis=0, keepdims=True)
    rows = table_ref.shape[0]
    hot = (iota((rows, text), 0) + me * rows == ids_ref[...]).astype(BF16)
    counts = dot_nt(jnp.ones((16, text), BF16), hot)
    pool = dot(counts.astype(BF16), table_ref[...])[0:1]
    temb_w = pool.shape[1]
    pq, mq = 384, 256
    pool = jnp.concatenate([pool, jnp.zeros((1, QUAD * pq - temb_w), F32)], axis=1)
    mean = jnp.concatenate([mean, jnp.zeros((1, QUAD * mq - width), F32)], axis=1)
    spread = jnp.concatenate([spread, jnp.zeros((1, QUAD * mq - width), F32)], axis=1)
    for q in range(QUAD):
        stat[q, :, 0:pq] = pool[:, q * pq : (q + 1) * pq]
        stat[q, :, pq : pq + mq] = mean[:, q * mq : (q + 1) * mq]
        stat[q, :, pq + mq : pq + 2 * mq] = spread[:, q * mq : (q + 1) * mq]

    first = [
        remote(stat.at[lax.rem(c + j, QUAD)], st1.at[j], s1_send.at[j], s1_recv.at[j], quad_to(j))
        for j in range(1, QUAD)
    ]
    for copy in first:
        copy.start()
    st1[0] = stat[c]

    per = width // GROUPS
    gr = jnp.floor((iota((width, width), 0).astype(F32) + 0.5) * (1.0 / per))
    gc = jnp.floor((iota((width, width), 1).astype(F32) + 0.5) * (1.0 / per))
    group[...] = (gr == gc).astype(BF16)
    half = temb_w // 2
    freq = jnp.exp(-math.log(10000.0) * iota((1, half), 1).astype(F32) / half)
    angle = time_ref[0].astype(F32) * freq
    temb = jnp.concatenate([jnp.cos(angle), jnp.sin(angle)], axis=1)

    def merge(ref, n):
        x = ref[...]
        count = x.shape[0]
        p = jnp.sum(x[:, :, 0:pq], axis=0)
        ms = x[:, :, pq : pq + mq]
        m = jnp.sum(ms, axis=0) * (1.0 / count)
        off = ms - m[None]
        v = jnp.sum(x[:, :, pq + mq : pq + 2 * mq], axis=0) + n * jnp.sum(off * off, axis=0)
        return p, m, v

    def put(ref, slot, three):
        p, m, v = three
        ref[slot, :, 0:pq] = p
        ref[slot, :, pq : pq + mq] = m
        ref[slot, :, pq + mq : pq + 2 * mq] = v

    for copy in first:
        copy.wait()
    put(st2, 0, merge(st1, float(tok)))
    second = [
        remote(st2.at[0], st2.at[j], s2_send.at[j], s2_recv.at[j], along(j)) for j in range(1, nz)
    ]
    for copy in second:
        copy.start()
    service(1)
    for copy in second:
        copy.wait()
    put(st3, c, merge(st2, float(tok * QUAD)))
    third = [
        remote(st3.at[c], st3.at[c], s3_send.at[j], s3_recv.at[j], quad_to(j))
        for j in range(1, QUAD)
    ]
    for copy in third:
        copy.start()
    service(2)
    for j in range(1, QUAD):
        third[j - 1].wait_send()
        owner = lax.rem(c + QUAD - j, QUAD)
        remote(st3.at[owner], st3.at[owner], s3_send.at[j], s3_recv.at[j], quad_from(j)).wait_recv()

    total = [st3[q] for q in range(QUAD)]
    pool = jnp.concatenate([t[:, 0:pq] for t in total], axis=1)[:, 0:temb_w]
    mean = jnp.concatenate([t[:, pq : pq + mq] for t in total], axis=1)[:, 0:width]
    spread = jnp.concatenate([t[:, pq + mq : pq + 2 * mq] for t in total], axis=1)[:, 0:width]

    cond = jax.nn.silu(temb + pool * (1.0 / text)).astype(BF16)
    loads[3].wait()
    shift = dot(jnp.broadcast_to(cond, (16, temb_w)), tw[...])[0:1]

    def group_mean(x):
        a, b, d = pieces(x)
        row = iota((16, width), 0)
        stacked = jnp.where(row == 0, a, jnp.where(row == 1, b, jnp.where(row == 2, d, 0.0)))
        return jnp.sum(dot(stacked.astype(BF16), group[...]), axis=0, keepdims=True) * (1.0 / per)

    service(1)
    centre = mean + shift
    centre_g = group_mean(centre)
    off = centre - centre_g
    var = group_mean(spread * (1.0 / (tok * QUAD * nz)) + off * off)
    scale = lax.rsqrt(var + 1e-5) * gain_ref[...].reshape(1, width)
    offset = (shift - centre_g) * scale + bias_ref[...].reshape(1, width)
    normed = (lat[...].astype(F32) * scale + offset).astype(BF16)
    service(1)

    loads[4].wait()
    qx[0] = dot_nt(wq[...], normed).astype(BF16)
    asks = [
        remote(qx.at[0], qx.at[j], q_send.at[j], q_recv.at[j], quad_to(j)) for j in range(1, QUAD)
    ]
    for copy in asks:
        copy.start()
    loads[5].wait()
    loads[6].wait()
    fk[...] = dot_nt(wk[...], normed).astype(BF16)
    fv[...] = dot_nt(wv[...], normed).astype(BF16)
    fresh_out = [
        pltpu.make_async_copy(fk, fk_hbm, out_sem.at[0]),
        pltpu.make_async_copy(fv, fv_hbm, out_sem.at[1]),
    ]
    for copy in fresh_out:
        copy.start()
    fill_keys(nz, dot_nt(eye(tok, tok), fk[...]).astype(BF16))
    kv[nz, pl.ds(att, att)] = fv[...]
    service(1)

    blank = jnp.zeros((64, tok), BF16)

    def place_queries(j):
        cols = pl.ds(j * tok, tok)
        for h in range(heads + 1):
            own = qx[j, min(h, 4) * 64 : min(h, 4) * 64 + 64]
            qp[h, 0:64, cols] = own if h % 2 == 0 else blank
            qp[h, 64:128, cols] = blank if h % 2 == 0 else own

    log2e = 0.125 * math.log2(math.e)

    def attend(h, q0, nq, parts, start):
        cols = pl.ds(q0, nq)
        count = sum(b - a for a, b in parts)

        def rows_of(r0, n):
            got = [kv[a:b, r0 : r0 + n].reshape((b - a) * n, LANE) for a, b in parts]
            return got[0] if len(got) == 1 else jnp.concatenate(got, axis=0)

        if h < 4:
            s = dot(rows_of((h // 2) * LANE, LANE), qp[h, :, cols])
        else:
            keys = rows_of(256, 64)
            early = dot(keys, qp[4, :, cols]).reshape(count, 64, nq)
            late = dot(keys, qp[5, :, cols]).reshape(count, 64, nq)
            s = jnp.concatenate([early, late], axis=1).reshape(count * tok, nq)
        m = jnp.max(s, axis=0, keepdims=True) * log2e
        if not start:
            old = top[h, 0:1, cols]
            m = jnp.maximum(old, m)
            fade = jnp.exp2(old - m)
        p = jnp.exp2(s * log2e - m).astype(BF16)
        r0 = att + h * 64
        values = [kv[i, r0 : r0 + 64] for a, b in parts for i in range(a, b)]
        values = values[0] if count == 1 else jnp.concatenate(values, axis=1)
        ones = jnp.ones((16, count * tok), BF16)
        out = dot(jnp.concatenate([values, ones], axis=0), p)[0:72]
        acc[h, :, cols] = out if start else acc[h, :, cols] * fade + out
        top[h, :, cols] = jnp.broadcast_to(m, (8, nq))

    reach_a = max(1, reach - 4)
    end_a = 2 * reach_a + 1
    ensure(2 * reach_a)
    place_queries(0)
    for h in range(heads):
        attend(h, 0, tok, [(nz, nz + 1), (1, end_a)], True)
    for copy in asks:
        copy.wait()
    for j in range(1, QUAD):
        place_queries(j)
    for h in range(heads):
        attend(h, tok, 3 * tok, [(0, end_a)], True)
        if h < 4:
            service(1)
    reach_b = reach - 2
    if reach_b > reach_a:
        end_b = 2 * reach_b + 1
        ensure(2 * reach_b)
        for h in range(heads):
            attend(h, 0, QUAD * tok, [(end_a, end_b)], False)
            if h % 2 == 1:
                service(1)
        end_a = end_b
    ensure(chunks)

    def finish(j, h):
        cols = pl.ds(j * tok, tok)
        weight = acc[h, 64:65, cols]
        return acc[h, 0:64, cols] / weight, top[h, 0:1, cols] + jnp.log2(weight)

    for h in range(heads):
        attend(h, tok, 3 * tok, [(end_a, nz)], False)
    replies = []
    row = iota((16, tok), 0)
    for j in range(1, QUAD):
        logs = jnp.zeros((16, tok), F32)
        for h in range(heads):
            o, log = finish(j, h)
            partial[j, h * 64 : h * 64 + 64] = o.astype(BF16)
            for i, x in enumerate(pieces(log)):
                logs = jnp.where(row == 3 * h + i, x, logs)
        partial[j, att : att + 16] = logs.astype(BF16)
        reply = remote(partial.at[j], arrived.at[j], o_send.at[j], o_recv.at[j], quad_from(j))
        reply.start()
        replies.append(reply)
    for h in range(heads):
        attend(h, 0, tok, [(end_a, nz)], False)
    own = [finish(0, h) for h in range(heads)]
    for reply in replies:
        reply.wait()
    attended = []
    peer_logs = [arrived[j, att : att + 16].astype(F32) for j in range(1, QUAD)]
    for h in range(heads):
        ls = [own[h][1]]
        for p in peer_logs:
            ls.append(p[3 * h : 3 * h + 1] + p[3 * h + 1 : 3 * h + 2] + p[3 * h + 2 : 3 * h + 3])
        os = [own[h][0]] + [arrived[j, h * 64 : h * 64 + 64].astype(F32) for j in range(1, QUAD)]
        big = jnp.maximum(jnp.maximum(ls[0], ls[1]), jnp.maximum(ls[2], ls[3]))
        ws = [jnp.exp2(x - big) for x in ls]
        num = ws[0] * os[0] + ws[1] * os[1] + ws[2] * os[2] + ws[3] * os[3]
        attended.append((num / (ws[0] + ws[1] + ws[2] + ws[3])).astype(BF16))
    attended = dot_nt(eye(tok, tok), jnp.concatenate(attended, axis=0)).astype(BF16)
    loads[7].wait()
    mixed[...] = (lat[...].astype(F32) + shift + dot(attended, wo[...])).astype(BF16)
    last = pltpu.make_async_copy(mixed, mixed_hbm, out_sem.at[2])
    last.start()
    for k in range(chunks):
        for up in (True, False):
            ring(k, up).wait_send()
    for copy in fresh_out:
        copy.wait()
    last.wait()


def solution(mesh):
    nz = mesh.shape["patch"] // QUAD

    def on_device(
        latents,
        stale_keys,
        stale_values,
        timestep,
        text_ids,
        text_table,
        time_weight,
        norm_gain,
        norm_bias,
        w_query,
        w_key,
        w_value,
        w_out,
    ):
        tok, width = latents.shape
        att = w_query.shape[1]
        temb_w = time_weight.shape[0]
        text = text_ids.shape[0]
        vmem = pl.BlockSpec(memory_space=pltpu.VMEM)
        smem = pl.BlockSpec(memory_space=pltpu.SMEM)
        hbm = pl.BlockSpec(memory_space=pl.ANY)
        chunks = nz - 1
        dma = pltpu.SemaphoreType.DMA
        scratch = [
            pltpu.VMEM((tok, width), BF16),
            pltpu.VMEM((att, tok), BF16),
            pltpu.VMEM((temb_w, width), BF16),
            pltpu.VMEM((att, width), BF16),
            pltpu.VMEM((att, width), BF16),
            pltpu.VMEM((att, width), BF16),
            pltpu.VMEM((att, width), BF16),
            pltpu.VMEM((nz + 1, 2 * att, tok), BF16),
            pltpu.VMEM((QUAD, 1, 896), F32),
            pltpu.VMEM((QUAD, 1, 896), F32),
            pltpu.VMEM((nz, 1, 896), F32),
            pltpu.VMEM((QUAD, 1, 896), F32),
            pltpu.VMEM((QUAD, att, tok), BF16),
            pltpu.VMEM((6, LANE, QUAD * tok), BF16),
            pltpu.VMEM((5, 72, QUAD * tok), F32),
            pltpu.VMEM((5, 8, QUAD * tok), F32),
            pltpu.VMEM((QUAD, att + 16, tok), BF16),
            pltpu.VMEM((QUAD, att + 16, tok), BF16),
            pltpu.VMEM((att, tok), BF16),
            pltpu.VMEM((att, tok), BF16),
            pltpu.VMEM((tok, width), BF16),
            pltpu.VMEM((width, width), BF16),
            dma((8,)),
            dma((3,)),
            dma((chunks,)),
            dma((chunks,)),
            dma((chunks,)),
            dma((chunks,)),
            dma((QUAD,)),
            dma((QUAD,)),
            dma((nz,)),
            dma((nz,)),
            dma((QUAD,)),
            dma((QUAD,)),
            dma((QUAD,)),
            dma((QUAD,)),
            dma((QUAD,)),
            dma((QUAD,)),
        ]
        mixed, fresh_keys, fresh_values = pl.pallas_call(
            functools.partial(kernel, nz, text),
            out_shape=(
                jax.ShapeDtypeStruct((tok, width), BF16),
                jax.ShapeDtypeStruct((att, tok), BF16),
                jax.ShapeDtypeStruct((att, tok), BF16),
            ),
            in_specs=[smem] + [vmem] * 4 + [hbm] * 8,
            out_specs=(hbm, hbm, hbm),
            scratch_shapes=scratch,
            compiler_params=pltpu.CompilerParams(
                collective_id=0, has_side_effects=True, vmem_limit_bytes=56 * 1024 * 1024
            ),
            cost_estimate=pl.CostEstimate(
                flops=2 * 10**9, bytes_accessed=6 * 10**6, transcendentals=6 * 10**6
            ),
        )(
            timestep,
            text_ids.reshape(1, text),
            text_table,
            norm_gain,
            norm_bias,
            latents,
            stale_keys.T,
            stale_values.T,
            time_weight,
            w_query.T,
            w_key.T,
            w_value.T,
            w_out,
        )
        return mixed, fresh_keys.T, fresh_values.T

    rows = P(("img", "patch"), None)
    return jax.shard_map(
        on_device,
        mesh=mesh,
        in_specs=(rows, rows, rows, P(), P("img"), P("patch", None)) + (P(),) * 7,
        out_specs=(rows, rows, rows),
        check_vma=False,
    )
```
